512 devices in a mesh: sector: 32 (over y, x), term: 16 (over z, core).
Axes of the slice: x: 4, y: 8, z: 8, core: 2. Of those that a mesh axis runs over, the one named last changes fastest.
Arguments:
- wavefunction: bfloat16 [64, 256, 256], P('sector', 'term'), as said below
- sector_sizes: int32 [64, 2], P('sector'), may hold values from 64 to 256, as said below
- term_shifts: int32 [128], P('term'), may hold values from -2 to 2
- left_blocks: bfloat16 [128, 64, 256, 256], P('term', 'sector')
- right_blocks: bfloat16 [128, 64, 256, 256], P('term', 'sector')
Outputs:
- sigma: float32 [64, 256, 256], P('sector', 'term')
- sigma_next: float32 [64, 256, 256], P('sector', 'term')
The draws below stay inside these ranges and needn't reach their ends.
Inputs may be any that keep to these rules, and one draw needn't show every extreme that they name: `sector_sizes`: in every draw one sector has 256 live rows and columns and another has 64 of both. `wavefunction`: entries outside a sector's live rows and columns are arbitrary.
All inputs are finite; a program needn't handle non-finite values.
Results may differ from the reference program's by a relative error of at most 0.0045.
Values may be sent and summed in bfloat16 or wider, within the bound.
A program may use at most 64 MiB of HBM per device.

```python
import math
import jax
import jax.numpy as jnp
from jax import lax

P_SIZE = 256
H = 2
S = 64
TERMS = 128


def shift_table(key):
    key = jax.random.fold_in(key, 101)
    key_shift, key_pick = jax.random.split(key)
    shifts = jax.random.randint(key_shift, (TERMS,), 0 - H, H + 1)
    picks = jax.random.permutation(key_pick, TERMS)
    index = jnp.arange(TERMS)
    shifts = jnp.where(index == picks[0], 0, shifts)
    shifts = jnp.where(index == picks[1], 0 - H, shifts)
    shifts = jnp.where(index == picks[2], H, shifts)
    return shifts.astype(jnp.int32)


def noise_block(key, scale):
    shape = (TERMS, S, P_SIZE, P_SIZE)
    values = jax.random.normal(key, shape, jnp.float32)
    return values * scale


def draw_term_shifts(key, part):
    return shift_table(key)


def draw_left_blocks(key, part):
    shifts = shift_table(key)
    key = jax.random.fold_in(key, 13)
    still = (shifts == 0).astype(jnp.float32)
    count = jnp.sum(still)
    noise = noise_block(key, 1.0 / math.sqrt(P_SIZE * TERMS))
    weight = still / count
    identity = jnp.eye(P_SIZE, dtype=jnp.float32)
    blocks = noise + weight[:, None, None, None] * identity[None, None, :, :]
    return blocks.astype(jnp.bfloat16)


def draw_right_blocks(key, part):
    key = jax.random.fold_in(key, 17)
    noise = noise_block(key, 1.0 / math.sqrt(P_SIZE))
    identity = jnp.eye(P_SIZE, dtype=jnp.float32)
    return (noise + identity[None, None, :, :]).astype(jnp.bfloat16)


def draw_wavefunction(key, part):
    key = jax.random.fold_in(key, 7)
    key_base, key_row, key_col = jax.random.split(key, 3)
    row_scale = jnp.exp(jax.random.uniform(key_row, (S, P_SIZE, 1), jnp.float32, math.log(0.3), math.log(3.0)))
    col_scale = jnp.exp(jax.random.uniform(key_col, (S, 1, P_SIZE), jnp.float32, math.log(0.3), math.log(3.0)))
    base = jax.random.normal(key_base, (S, P_SIZE, P_SIZE), jnp.float32)
    return (base * row_scale * col_scale).astype(jnp.bfloat16)


def draw_sector_sizes(key, part):
    key = jax.random.fold_in(key, 11)
    key_base, key_top, key_low = jax.random.split(key, 3)
    base = jax.random.randint(key_base, (S, 2), P_SIZE // 4, P_SIZE + 1)
    top = jax.random.randint(key_top, (), 0, S)
    low = (top + 1 + jax.random.randint(key_low, (), 0, S - 1)) % S
    index = jnp.arange(S)[:, None]
    base = jnp.where(index == top, P_SIZE, base)
    base = jnp.where(index == low, P_SIZE // 4, base)
    return base.astype(jnp.int32)


def setup_inputs(seed: int = 0) -> dict:
    keys = jax.random.split(jax.random.key(seed), 6)
    return {
        "wavefunction": draw_wavefunction(jax.random.fold_in(keys[5], 71), 0),
        "sector_sizes": draw_sector_sizes(jax.random.fold_in(keys[5], 71), 0),
        "term_shifts": draw_term_shifts(jax.random.fold_in(keys[5], 71), 0),
        "left_blocks": draw_left_blocks(jax.random.fold_in(keys[5], 71), 0),
        "right_blocks": draw_right_blocks(jax.random.fold_in(keys[5], 71), 0),
    }


def live_mask(sector_sizes):
    index = jnp.arange(P_SIZE, dtype=jnp.int32)
    rows_live = index[None, :, None] < sector_sizes[:, 0][:, None, None]
    cols_live = index[None, None, :] < sector_sizes[:, 1][:, None, None]
    return (rows_live & cols_live).astype(jnp.float32)


def apply_hamiltonian(vector, term_shifts, left_blocks, right_blocks, live):
    zero_pad = jnp.zeros((H, P_SIZE, P_SIZE), vector.dtype)
    padded = jnp.concatenate([zero_pad, vector, zero_pad], axis=0)

    def one_sector(sector_idx):
        source = (sector_idx + H - term_shifts).astype(jnp.int32)
        sources = padded[source]
        left = left_blocks[:, sector_idx].astype(jnp.float32)
        right = right_blocks[:, sector_idx].astype(jnp.float32)
        mixed = jnp.einsum('tij,tjk->tik', left, sources.astype(jnp.float32)).astype(jnp.bfloat16)
        total = jnp.einsum('tik,tlk->il', mixed.astype(jnp.float32), right)
        return total * live[sector_idx]

    return lax.map(one_sector, jnp.arange(S, dtype=jnp.int32))


def reference(wavefunction, sector_sizes, term_shifts, left_blocks, right_blocks):
    live = live_mask(sector_sizes)
    psi_live = (wavefunction.astype(jnp.float32) * live).astype(jnp.bfloat16)
    sigma = apply_hamiltonian(psi_live, term_shifts, left_blocks, right_blocks, live)
    psi_wide = psi_live.astype(jnp.float32)
    theta = jnp.sum(psi_wide * sigma) / jnp.sum(psi_wide * psi_wide)
    residual = (sigma - theta * psi_wide).astype(jnp.bfloat16)
    sigma_next = apply_hamiltonian(residual, term_shifts, left_blocks, right_blocks, live)
    return sigma, sigma_next
```

```python
import functools

import jax
import jax.numpy as jnp
from jax import lax
from jax.experimental import pallas as pl
from jax.experimental.pallas import tpu as pltpu
from jax.sharding import PartitionSpec as P

H = 2
MESH = pl.DeviceIdType.MESH
F32, BF16 = jnp.float32, jnp.bfloat16
INNER = 4


class Sems:
    def __init__(self, send, recv):
        self.send, self.recv, self.count = send, recv, 0

    def take(self):
        self.count += 1
        return self.count - 1


def kernel(
    dims, psi_ref, sizes_ref, shifts_ref, left_hbm, right_hbm, sigma_ref, next_ref,
    left, right, v0, v1, mixed, total, peer, chunk, landed, th_own, th_z, th_x, th_y,
    load_sem, send_sem, recv_sem,
):
    n_sector, n_term = dims
    nz = n_term // 2
    n_outer = n_sector // INNER
    terms, width = left.shape[0], left.shape[-1]
    rows = psi_ref.shape[1]
    s, t = lax.axis_index("sector"), lax.axis_index("term")
    z, c = t // 2, t % 2
    sx, sy = s % INNER, s // INNER
    other = 1 - c
    has_lo, has_hi = s > 0, s < n_sector - 1
    sems = Sems(send_sem, recv_sem)
    sent = []

    def at_z(d):
        return lax.rem(z + d, nz)

    def dev(sector, zz, core):
        return (sector, zz * 2 + core)

    def remote(src, dst, idx, device):
        return pltpu.make_async_remote_copy(
            src_ref=src, dst_ref=dst, send_sem=send_sem.at[idx], recv_sem=recv_sem.at[idx],
            device_id=device, device_id_type=MESH,
        )

    def send(src, dst, idx, device, when=None):
        copy = remote(src, dst, idx, device)
        if when is None:
            copy.start()
        else:
            pl.when(when)(copy.start)
        sent.append((copy, when))

    def arrive(dst, idx, when=None):
        copy = remote(dst, dst, idx, dev(s, z, other))
        if when is None:
            copy.wait_recv()
        else:
            pl.when(when)(copy.wait_recv)

    loads = []
    loads.append(pltpu.make_async_copy(left_hbm, left, load_sem.at[0]))
    for k in range(terms):
        for i in range(2):
            loads.append(
                pltpu.make_async_copy(
                    right_hbm.at[k, i], right.at[i, :, pl.ds(k * width, width)],
                    load_sem.at[1 + 2 * k + i],
                )
            )
    for load in loads:
        load.start()

    barrier = pltpu.get_barrier_semaphore()

    def greet(device):
        pl.semaphore_signal(barrier, inc=1, device_id=device, device_id_type=MESH)

    greet(dev(s, z, other))
    for d in range(1, nz):
        greet(dev(s, at_z(d), c))
    for d in range(1, INNER):
        greet(dev(sy * INNER + lax.rem(sx + d, INNER), z, c))
    for d in range(1, n_outer):
        greet(dev(lax.rem(sy + d, n_outer) * INNER + sx, z, c))
    lo_cross = jnp.logical_and(has_lo, sx == 0)
    hi_cross = jnp.logical_and(has_hi, sx == INNER - 1)
    pl.when(lo_cross)(lambda: greet(dev(s - 1, z, c)))
    pl.when(hi_cross)(lambda: greet(dev(s + 1, z, c)))

    def live(i):
        row = lax.broadcasted_iota(jnp.int32, (rows, width), 0) + t * rows
        col = lax.broadcasted_iota(jnp.int32, (rows, width), 1)
        return jnp.logical_and(row < sizes_ref[i, 0], col < sizes_ref[i, 1])

    lives = [live(i) for i in range(2)]
    squares = jnp.zeros((8, 128), F32)

    def fold(x):
        x = x.reshape(-1, 8, width).sum(axis=0)
        return functools.reduce(jnp.add, [x[:, k : k + 128] for k in range(0, width, 128)])

    for i in range(2):
        own = jnp.where(lives[i], psi_ref[i].astype(F32), 0.0)
        v0[2 + i, z, c] = own.astype(BF16)
        squares += fold(own * own)

    @pl.when(jnp.logical_not(has_lo))
    def _():
        v0[0:2] = jnp.zeros((2, nz, 2, rows, width), BF16)
        v1[0:2] = jnp.zeros((2, nz, 2, rows, width), BF16)

    @pl.when(jnp.logical_not(has_hi))
    def _():
        v0[4:6] = jnp.zeros((2, nz, 2, rows, width), BF16)
        v1[4:6] = jnp.zeros((2, nz, 2, rows, width), BF16)

    pl.semaphore_wait(
        barrier,
        1 + (nz - 1) + (INNER - 1) + (n_outer - 1)
        + lo_cross.astype(jnp.int32) + hi_cross.astype(jnp.int32),
    )

    order = []
    for d in range(1, nz // 2 + 1):
        order.append(d)
        if nz - d != d:
            order.append(nz - d)

    def gather(v):
        zi = [sems.take() for _ in range(nz)]
        lo = [sems.take() for _ in range(nz)]
        hi = [sems.take() for _ in range(nz)]
        sib = [sems.take() for _ in range(3)]
        mid = pl.ds(2, 2)
        for d in order:
            send(v.at[mid, z, c], v.at[mid, z, c], zi[d], dev(s, at_z(d), c))
        for d in [0] + order:
            zz = at_z(nz - d) if d else z
            block = v.at[mid, zz, c]
            if d:
                arrive(block, zi[d])
            send(block, v.at[pl.ds(4, 2), zz, c], lo[d], dev(s - 1, z, c), has_lo)
            send(block, v.at[pl.ds(0, 2), zz, c], hi[d], dev(s + 1, z, c), has_hi)
        whole = [v.at[pl.ds(2 * k, 2), :, c] for k in range(3)]
        back = [v.at[pl.ds(2 * k, 2), :, other] for k in range(3)]
        send(whole[1], whole[1], sib[1], dev(s, z, other))
        for d in [0] + order:
            zz = at_z(nz - d) if d else z
            arrive(v.at[pl.ds(0, 2), zz, c], hi[d], has_lo)
            arrive(v.at[pl.ds(4, 2), zz, c], lo[d], has_hi)
        send(whole[0], whole[0], sib[0], dev(s, z, other), has_lo)
        send(whole[2], whole[2], sib[2], dev(s, z, other), has_hi)
        arrive(back[1], sib[1])
        arrive(back[0], sib[0], has_lo)
        arrive(back[2], sib[2], has_hi)

    def first_half(v, i):
        for k in range(terms):
            block = v[i + H - shifts_ref[k]].reshape(width, width)
            out = jnp.dot(left[k, i], block, preferred_element_type=F32)
            mixed[:, k * width : (k + 1) * width] = out.astype(BF16)

    def second_half(r, i):
        out = lax.dot_general(
            mixed[...], right[i], (((1,), (1,)), ((), ())), preferred_element_type=F32
        )
        total[r, i] = out.reshape(nz, 2, rows, width)
        return out

    def swap(r, i, idx):
        send(total.at[r, i, :, other], peer.at[r, i], idx, dev(s, z, other))

    def scatter(r, i, idx, zi):
        arrive(peer.at[r, i], idx)
        chunk[r, i] = (total[r, i, :, c] + peer[r, i]).astype(chunk.dtype)
        for d in order:
            zz = at_z(d)
            send(chunk.at[r, i, zz], landed.at[r, i, z], zi[d], dev(s, zz, c))

    def collect(r, i, zi):
        acc = total[r, i, z, c] + peer[r, i, z]
        for d in order:
            zz = at_z(nz - d)
            arrive(landed.at[r, i, zz], zi[d])
            acc = acc + landed[r, i, zz].astype(F32)
        return jnp.where(lives[i], acc, 0.0)

    def product(r, v):
        gather(v)
        swaps = [sems.take() for _ in range(2)]
        zis = [[sems.take() for _ in range(nz)] for _ in range(2)]
        if r == 0:
            for load in loads:
                load.wait()
        outs = []
        first_half(v, 0)
        outs.append(second_half(r, 0))
        swap(r, 0, swaps[0])
        inner = fold(outs[0] * v0[2].reshape(width, width).astype(F32)) if r == 0 else None
        first_half(v, 1)
        scatter(r, 0, swaps[0], zis[0])
        outs.append(second_half(r, 1))
        swap(r, 1, swaps[1])
        if r == 0:
            inner += fold(outs[1] * v0[3].reshape(width, width).astype(F32))
            theta_start(inner)
        scatter(r, 1, swaps[1], zis[1])
        theta = theta_end() if r == 0 else None
        return [collect(r, i, zis[i]) for i in range(2)], theta

    tz = [sems.take() for _ in range(n_term)]
    tx = [sems.take() for _ in range(INNER)]
    ty = [sems.take() for _ in range(n_outer)]

    def theta_start(inner):
        th_own[0] = jnp.concatenate([inner[:4] + inner[4:], squares[:4] + squares[4:]], axis=0)
        for d in range(1, n_term):
            send(th_own.at[0], th_z.at[d], tz[d], (s, lax.rem(t + d, n_term)))

    def theta_end():
        def summed(own, slots, idx, n):
            acc = own
            for d in range(1, n):
                arrive(slots.at[d], idx[d])
                acc = acc + slots[d]
            return acc

        th_own[1] = summed(th_own[0], th_z, tz, n_term)
        for d in range(1, INNER):
            send(th_own.at[1], th_x.at[d], tx[d], (sy * INNER + lax.rem(sx + d, INNER), t))
        th_own[2] = summed(th_own[1], th_x, tx, INNER)
        for d in range(1, n_outer):
            send(th_own.at[2], th_y.at[d], ty[d], (lax.rem(sy + d, n_outer) * INNER + sx, t))
        both = summed(th_own[2], th_y, ty, n_outer)
        num = jnp.sum(both[:4], keepdims=True)
        den = jnp.sum(both[4:], keepdims=True)
        return num / den

    sigma, theta = product(0, v0)
    for i in range(2):
        sigma_ref[i] = sigma[i]
        psi = v0[2 + i, z, c].astype(F32)
        v1[2 + i, z, c] = (sigma[i] - theta * psi).astype(BF16)
    last, _ = product(1, v1)
    for i in range(2):
        next_ref[i] = last[i]
    for copy, when in sent:
        if when is None:
            copy.wait_send()
        else:
            pl.when(when)(copy.wait_send)
    assert sems.count <= send_sem.shape[0]


def solution(mesh, link=BF16):
    dims = (mesh.shape["sector"], mesh.shape["term"])

    def step(psi, sizes, shifts, left, right):
        n_sector, n_term = dims
        nz = n_term // 2
        terms, width, rows = left.shape[0], left.shape[-1], psi.shape[1]
        n_sems = 2 * (3 * nz + 3 + 2 + 2 * nz) + n_term + INNER + n_sector // INNER
        out = jax.ShapeDtypeStruct((2, rows, width), F32)
        vmem, smem = (pl.BlockSpec(memory_space=m) for m in (pltpu.VMEM, pltpu.SMEM))
        hbm = pl.BlockSpec(memory_space=pl.ANY)
        return pl.pallas_call(
            functools.partial(kernel, dims),
            out_shape=(out, out),
            in_specs=[vmem, smem, smem, hbm, hbm],
            out_specs=(vmem, vmem),
            scratch_shapes=[
                pltpu.VMEM((terms, 2, width, width), BF16),
                pltpu.VMEM((2, width, terms * width), BF16),
                pltpu.VMEM((6, nz, 2, rows, width), BF16),
                pltpu.VMEM((6, nz, 2, rows, width), BF16),
                pltpu.VMEM((width, terms * width), BF16),
                pltpu.VMEM((2, 2, nz, 2, rows, width), F32),
                pltpu.VMEM((2, 2, nz, rows, width), F32),
                pltpu.VMEM((2, 2, nz, rows, width), link),
                pltpu.VMEM((2, 2, nz, rows, width), link),
                pltpu.VMEM((3, 8, 128), F32),
                pltpu.VMEM((n_term, 8, 128), F32),
                pltpu.VMEM((INNER, 8, 128), F32),
                pltpu.VMEM((n_sector // INNER, 8, 128), F32),
                pltpu.SemaphoreType.DMA((1 + 2 * terms,)),
                pltpu.SemaphoreType.DMA((n_sems,)),
                pltpu.SemaphoreType.DMA((n_sems,)),
            ],
            compiler_params=pltpu.CompilerParams(
                collective_id=0, has_side_effects=True, vmem_limit_bytes=62 * 2**20
            ),
            cost_estimate=pl.CostEstimate(
                flops=8 * terms * width**3 * 2, bytes_accessed=4 * terms * width * width * 2,
                transcendentals=0,
            ),
        )(psi, sizes, shifts, left, right)

    return jax.shard_map(
        step,
        mesh=mesh,
        in_specs=(
            P("sector", "term", None),
            P("sector", None),
            P("term"),
            P("term", "sector", None, None),
            P("term", "sector", None, None),
        ),
        out_specs=(P("sector", "term", None), P("sector", "term", None)),
        check_vma=False,
    )
```

```python
import functools

import jax
import jax.numpy as jnp
from jax import lax
from jax.experimental import pallas as pl
from jax.experimental.pallas import tpu as pltpu
from jax.sharding import PartitionSpec as P

H = 2
MESH = pl.DeviceIdType.MESH
F32, BF16 = jnp.float32, jnp.bfloat16
INNER = 4


class Sems:
    def __init__(self, send, recv):
        self.send, self.recv, self.count = send, recv, 0

    def take(self):
        self.count += 1
        return self.count - 1


def kernel(
    dims, psi_hbm, sizes_ref, shifts_ref, left_hbm, right_hbm, sigma_hbm, next_hbm,
    psi_ref, outs, left, right, v0, v1, v2, mixed, total, peer, chunk, landed,
    th_own, th_z, th_x, th_y, th_side, load_sem, send_sem, recv_sem,
):
    n_sector, n_term = dims
    nz = n_term // 2
    n_outer = n_sector // INNER
    terms, width = left.shape[0], left.shape[-1]
    rows = psi_ref.shape[1]
    s, t = lax.axis_index("sector"), lax.axis_index("term")
    z, c = t // 2, t % 2
    sx, sy = s % INNER, s // INNER
    other = 1 - c
    has_lo, has_hi = s > 0, s < n_sector - 1
    sems = Sems(send_sem, recv_sem)
    sent = []

    def at_z(d):
        return lax.rem(z + d, nz)

    def dev(sector, zz, core):
        return (sector, zz * 2 + core)

    def remote(src, dst, idx, device):
        return pltpu.make_async_remote_copy(
            src_ref=src, dst_ref=dst, send_sem=send_sem.at[idx], recv_sem=recv_sem.at[idx],
            device_id=device, device_id_type=MESH,
        )

    def send(src, dst, idx, device, when=None):
        copy = remote(src, dst, idx, device)
        if when is None:
            copy.start()
        else:
            pl.when(when)(copy.start)
        sent.append((copy, when))

    def arrive(dst, idx, when=None):
        copy = remote(dst, dst, idx, dev(s, z, other))
        if when is None:
            copy.wait_recv()
        else:
            pl.when(when)(copy.wait_recv)

    own_load = pltpu.make_async_copy(psi_hbm, psi_ref, load_sem.at[0])
    own_load.start()
    loads = []
    loads.append(pltpu.make_async_copy(left_hbm, left, load_sem.at[1]))
    for k in range(terms):
        for i in range(2):
            loads.append(
                pltpu.make_async_copy(
                    right_hbm.at[k, i], right.at[i, :, pl.ds(k * width, width)],
                    load_sem.at[2 + 2 * k + i],
                )
            )
    for load in loads:
        load.start()

    barrier = pltpu.get_barrier_semaphore()

    def greet(device):
        pl.semaphore_signal(barrier, inc=1, device_id=device, device_id_type=MESH)

    greet(dev(s, z, other))
    for d in range(1, nz):
        greet(dev(s, at_z(d), c))
    for d in range(1, INNER):
        greet(dev(sy * INNER + lax.rem(sx + d, INNER), z, c))
    for d in range(1, n_outer):
        greet(dev(lax.rem(sy + d, n_outer) * INNER + sx, z, c))
    lo_cross = jnp.logical_and(has_lo, sx == 0)
    hi_cross = jnp.logical_and(has_hi, sx == INNER - 1)
    pl.when(lo_cross)(lambda: greet(dev(s - 1, z, c)))
    pl.when(hi_cross)(lambda: greet(dev(s + 1, z, c)))

    def live(i):
        row = lax.broadcasted_iota(jnp.int32, (rows, width), 0) + t * rows
        col = lax.broadcasted_iota(jnp.int32, (rows, width), 1)
        return jnp.logical_and(row < sizes_ref[i, 0], col < sizes_ref[i, 1])

    own_load.wait()
    lives = [live(i) for i in range(2)]
    squares = jnp.zeros((8, 128), F32)

    def fold(x):
        x = x.reshape(-1, 8, width).sum(axis=0)
        return functools.reduce(jnp.add, [x[:, k : k + 128] for k in range(0, width, 128)])

    for i in range(2):
        own = jnp.where(lives[i], psi_ref[i].astype(F32), 0.0)
        v0[2 + i, z, c] = own.astype(BF16)
        squares += fold(own * own)

    @pl.when(jnp.logical_not(has_lo))
    def _():
        v0[0:2] = jnp.zeros((2, nz, 2, rows, width), BF16)
        v1[0:2] = jnp.zeros((2, nz, 2, rows, width), BF16)
        th_side[0] = jnp.zeros((8, 128), F32)

    @pl.when(jnp.logical_not(has_hi))
    def _():
        v0[4:6] = jnp.zeros((2, nz, 2, rows, width), BF16)
        v1[4:6] = jnp.zeros((2, nz, 2, rows, width), BF16)
        th_side[1] = jnp.zeros((8, 128), F32)

    pl.semaphore_wait(
        barrier,
        1 + (nz - 1) + (INNER - 1) + (n_outer - 1)
        + lo_cross.astype(jnp.int32) + hi_cross.astype(jnp.int32),
    )

    order = []
    for d in range(1, nz // 2 + 1):
        order.append(d)
        if nz - d != d:
            order.append(nz - d)

    def gather(v, meanwhile=None):
        zi = [sems.take() for _ in range(nz)]
        lo = [sems.take() for _ in range(nz)]
        hi = [sems.take() for _ in range(nz)]
        sib = [sems.take() for _ in range(3)]
        mid, low, high = pl.ds(2, 2), pl.ds(0, 2), pl.ds(4, 2)
        own = v.at[mid, z, c]
        for d in reversed(order):
            send(own, own, zi[d], dev(s, at_z(d), c))
        for d in [0] + order:
            zz = at_z(nz - d) if d else z
            block = v.at[mid, zz, c]
            if d:
                arrive(block, zi[d])
            send(block, v.at[high, zz, c], lo[d], dev(s - 1, z, c), has_lo)
            send(block, v.at[low, zz, c], hi[d], dev(s + 1, z, c), has_hi)
            if d == 0 and meanwhile is not None:
                meanwhile()
        whole = [v.at[pl.ds(2 * k, 2), :, c] for k in range(3)]
        back = [v.at[pl.ds(2 * k, 2), :, other] for k in range(3)]
        send(whole[1], whole[1], sib[1], dev(s, z, other))
        for d in [0] + order:
            zz = at_z(nz - d) if d else z
            arrive(v.at[pl.ds(0, 2), zz, c], hi[d], has_lo)
            arrive(v.at[pl.ds(4, 2), zz, c], lo[d], has_hi)
        send(whole[0], whole[0], sib[0], dev(s, z, other), has_lo)
        send(whole[2], whole[2], sib[2], dev(s, z, other), has_hi)
        arrive(back[1], sib[1])
        arrive(back[0], sib[0], has_lo)
        arrive(back[2], sib[2], has_hi)

    def first_half(v, i):
        for k in range(terms):
            block = v[i + H - shifts_ref[k]].reshape(width, width)
            out = jnp.dot(left[k, i], block, preferred_element_type=F32)
            mixed[:, k * width : (k + 1) * width] = out.astype(BF16)

    def second_half(r, i):
        out = lax.dot_general(
            mixed[...], right[i], (((1,), (1,)), ((), ())), preferred_element_type=F32
        )
        total[r, i] = out.reshape(nz, 2, rows, width)
        return out

    def swap(r, i, idx):
        send(total.at[r, i, :, other], peer.at[r, i], idx, dev(s, z, other))

    def scatter(r, i, idx, zi):
        arrive(peer.at[r, i], idx)
        chunk[r, i] = (total[r, i, :, c] + peer[r, i]).astype(chunk.dtype)
        for d in order:
            zz = at_z(d)
            send(chunk.at[r, i, zz], landed.at[r, i, z], zi[d], dev(s, zz, c))

    def collect(r, i, zi):
        acc = total[r, i, z, c] + peer[r, i, z]
        for d in order:
            zz = at_z(nz - d)
            arrive(landed.at[r, i, zz], zi[d])
            acc = acc + landed[r, i, zz].astype(F32)
        return jnp.where(lives[i], acc, 0.0)

    def product(r, v, src):
        swaps = [sems.take() for _ in range(2)]
        zis = [[sems.take() for _ in range(nz)] for _ in range(2)]
        if r == 0:
            for load in loads:
                load.wait()
        first_half(src, 0)
        out = second_half(r, 0)
        swap(r, 0, swaps[0])
        if r == 0:
            inner = fold(out * v0[2].reshape(width, width).astype(F32))
        first_half(src, 1)
        scatter(r, 0, swaps[0], zis[0])
        out = second_half(r, 1)
        swap(r, 1, swaps[1])
        if r == 0:
            inner += fold(out * v0[3].reshape(width, width).astype(F32))
            theta_start(inner)
        scatter(r, 1, swaps[1], zis[1])
        quotient = theta_column() if r == 0 else None
        return [collect(r, i, zis[i]) for i in range(2)], quotient

    tz = [sems.take() for _ in range(n_term)]
    tx = [sems.take() for _ in range(INNER)]
    ty = [sems.take() for _ in range(n_outer)]
    ts = [sems.take() for _ in range(2)]

    def summed(own, slots, idx):
        acc = own
        for d in range(1, len(idx)):
            arrive(slots.at[d], idx[d])
            acc = acc + slots[d]
        return acc

    def ratio(both):
        return jnp.sum(both[:4], keepdims=True) / jnp.sum(both[4:], keepdims=True)

    def column_ratio(both):
        value = ratio(both)
        return jnp.where(jnp.abs(value) < 1e30, value, 0.0)

    def theta_start(inner):
        th_own[0] = jnp.concatenate([inner[:4] + inner[4:], squares[:4] + squares[4:]], axis=0)
        for d in range(1, n_term):
            send(th_own.at[0], th_z.at[d], tz[d], (s, lax.rem(t + d, n_term)))

    def theta_column():
        both = summed(th_own[0], th_z, tz)
        th_own[1] = both
        for d in range(1, INNER):
            send(th_own.at[1], th_x.at[d], tx[d], (sy * INNER + lax.rem(sx + d, INNER), t))
        send(th_own.at[1], th_side.at[1], ts[1], dev(s - 1, z, c), has_lo)
        send(th_own.at[1], th_side.at[0], ts[0], dev(s + 1, z, c), has_hi)
        return column_ratio(both)

    def theta_across():
        th_own[2] = summed(th_own[1], th_x, tx)
        for d in range(1, n_outer):
            send(th_own.at[2], th_y.at[d], ty[d], (lax.rem(sy + d, n_outer) * INNER + sx, t))

    def theta_end():
        theta = ratio(summed(th_own[2], th_y, ty))
        arrive(th_side.at[0], ts[0], has_lo)
        arrive(th_side.at[1], ts[1], has_hi)
        return theta, column_ratio(th_side[0]), column_ratio(th_side[1])
    gather(v0)
    sigma, quotient = product(0, v0, v0)
    for i in range(2):
        outs[0, i] = sigma[i]
        psi = v0[2 + i, z, c].astype(F32)
        v1[2 + i, z, c] = (sigma[i] - quotient * psi).astype(BF16)
    sigma_out = pltpu.make_async_copy(outs.at[0], sigma_hbm, load_sem.at[0])
    sigma_out.start()
    gather(v1, theta_across)
    theta, below, above = theta_end()
    for j in range(6):
        change = (below, quotient, above)[j // 2] - theta
        v2[j] = (v1[j].astype(F32) + change * v0[j].astype(F32)).astype(BF16)
    last, _ = product(1, v1, v2)
    for i in range(2):
        outs[1, i] = last[i]
    next_out = pltpu.make_async_copy(outs.at[1], next_hbm, load_sem.at[1])
    next_out.start()
    sigma_out.wait()
    next_out.wait()
    for copy, when in sent:
        if when is None:
            copy.wait_send()
        else:
            pl.when(when)(copy.wait_send)
    assert sems.count <= send_sem.shape[0]


def solution(mesh, link=BF16):
    dims = (mesh.shape["sector"], mesh.shape["term"])

    def step(psi, sizes, shifts, left, right):
        n_sector, n_term = dims
        nz = n_term // 2
        terms, width, rows = left.shape[0], left.shape[-1], psi.shape[1]
        n_sems = 2 * (3 * nz + 3 + 2 + 2 * nz) + n_term + INNER + n_sector // INNER + 2
        out = jax.ShapeDtypeStruct((2, rows, width), F32)
        smem = pl.BlockSpec(memory_space=pltpu.SMEM)
        hbm = pl.BlockSpec(memory_space=pl.ANY)
        return pl.pallas_call(
            functools.partial(kernel, dims),
            out_shape=(out, out),
            in_specs=[hbm, smem, smem, hbm, hbm],
            out_specs=(hbm, hbm),
            scratch_shapes=[
                pltpu.VMEM((2, rows, width), BF16),
                pltpu.VMEM((2, 2, rows, width), F32),
                pltpu.VMEM((terms, 2, width, width), BF16),
                pltpu.VMEM((2, width, terms * width), BF16),
                pltpu.VMEM((6, nz, 2, rows, width), BF16),
                pltpu.VMEM((6, nz, 2, rows, width), BF16),
                pltpu.VMEM((6, nz, 2, rows, width), BF16),
                pltpu.VMEM((width, terms * width), BF16),
                pltpu.VMEM((2, 2, nz, 2, rows, width), F32),
                pltpu.VMEM((2, 2, nz, rows, width), F32),
                pltpu.VMEM((2, 2, nz, rows, width), link),
                pltpu.VMEM((2, 2, nz, rows, width), link),
                pltpu.VMEM((3, 8, 128), F32),
                pltpu.VMEM((n_term, 8, 128), F32),
                pltpu.VMEM((INNER, 8, 128), F32),
                pltpu.VMEM((n_sector // INNER, 8, 128), F32),
                pltpu.VMEM((2, 8, 128), F32),
                pltpu.SemaphoreType.DMA((2 + 2 * terms,)),
                pltpu.SemaphoreType.DMA((n_sems,)),
                pltpu.SemaphoreType.DMA((n_sems,)),
            ],
            compiler_params=pltpu.CompilerParams(
                collective_id=0, has_side_effects=True, vmem_limit_bytes=62 * 2**20
            ),
            cost_estimate=pl.CostEstimate(
                flops=8 * terms * width**3 * 2, bytes_accessed=4 * terms * width * width * 2,
                transcendentals=0,
            ),
        )(psi, sizes, shifts, left, right)

    return jax.shard_map(
        step,
        mesh=mesh,
        in_specs=(
            P("sector", "term", None),
            P("sector", None),
            P("term"),
            P("term", "sector", None, None),
            P("term", "sector", None, None),
        ),
        out_specs=(P("sector", "term", None), P("sector", "term", None)),
        check_vma=False,
    )
```

```python
import functools

import jax
import jax.numpy as jnp
from jax import lax
from jax.experimental import pallas as pl
from jax.experimental.pallas import tpu as pltpu
from jax.sharding import PartitionSpec as P

H = 2
MESH = pl.DeviceIdType.MESH
F32, BF16 = jnp.float32, jnp.bfloat16
INNER = 4


class Sems:
    def __init__(self, sems):
        self.sems, self.count = sems, 0

    def take(self):
        self.count += 1
        return self.sems.at[self.count - 1]


def kernel(
    dims, psi_hbm, sizes_ref, shifts_ref, left_hbm, right_hbm, sigma_hbm, next_hbm,
    psi_ref, outs, left, right, v0, v1, v2, mixed, total, peer, chunk, landed,
    th_own, th_z, th_x, th_y, th_side, load_sem, send_sem, recv_sem,
):
    n_sector, n_term = dims
    nz = n_term // 2
    n_outer = n_sector // INNER
    terms, width = left.shape[0], left.shape[-1]
    rows = psi_ref.shape[1]
    s, t = lax.axis_index("sector"), lax.axis_index("term")
    z, c = t // 2, t % 2
    sx, sy = s % INNER, s // INNER
    other = 1 - c
    has_lo, has_hi = s > 0, s < n_sector - 1
    sends, recvs = Sems(send_sem), Sems(recv_sem)
    sent = []

    def at_z(d):
        return lax.rem(z + d, nz)

    def dev(sector, zz, core):
        return (sector, zz * 2 + core)

    def guarded(when, act):
        if when is None:
            act()
        else:
            pl.when(when)(act)

    def remote(src, dst, out_sem, in_sem, device):
        return pltpu.make_async_remote_copy(
            src_ref=src, dst_ref=dst, send_sem=out_sem, recv_sem=in_sem,
            device_id=device, device_id_type=MESH,
        )

    def send(src, dst, group, device):
        out_sem, in_sem, when = group
        guarded(when, remote(src, dst, out_sem, in_sem, device).start)

    def group(region, when=None):
        out_sem, in_sem = sends.take(), recvs.take()
        sent.append((remote(region, region, out_sem, in_sem, dev(s, z, other)), when))
        return out_sem, in_sem, when

    def arrive(region, in_sem, when=None):
        copy = remote(region, region, send_sem.at[0], in_sem, dev(s, z, other))
        guarded(when, copy.wait_recv)

    own_load = pltpu.make_async_copy(psi_hbm, psi_ref, load_sem.at[0])
    own_load.start()
    pltpu.make_async_copy(left_hbm, left, load_sem.at[1]).start()
    for k in range(terms):
        for i in range(2):
            pltpu.make_async_copy(
                right_hbm.at[k, i], right.at[i, :, pl.ds(k * width, width)], load_sem.at[2]
            ).start()

    barrier = pltpu.get_barrier_semaphore()

    def greet(device):
        pl.semaphore_signal(barrier, inc=1, device_id=device, device_id_type=MESH)

    greet(dev(s, z, other))
    for d in range(1, nz):
        greet(dev(s, at_z(d), c))
    for d in range(1, INNER):
        greet(dev(sy * INNER + lax.rem(sx + d, INNER), z, c))
    for d in range(1, n_outer):
        greet(dev(lax.rem(sy + d, n_outer) * INNER + sx, z, c))
    lo_cross = jnp.logical_and(has_lo, sx == 0)
    hi_cross = jnp.logical_and(has_hi, sx == INNER - 1)
    pl.when(lo_cross)(lambda: greet(dev(s - 1, z, c)))
    pl.when(hi_cross)(lambda: greet(dev(s + 1, z, c)))

    def live(i):
        row = lax.broadcasted_iota(jnp.int32, (rows, width), 0) + t * rows
        col = lax.broadcasted_iota(jnp.int32, (rows, width), 1)
        return jnp.logical_and(row < sizes_ref[i, 0], col < sizes_ref[i, 1])

    own_load.wait()
    lives = [live(i) for i in range(2)]
    squares = jnp.zeros((8, 128), F32)

    def fold(x):
        x = x.reshape(-1, 8, width).sum(axis=0)
        return functools.reduce(jnp.add, [x[:, k : k + 128] for k in range(0, width, 128)])

    for i in range(2):
        own = jnp.where(lives[i], psi_ref[i].astype(F32), 0.0)
        v0[2 + i, z, c] = own.astype(BF16)
        squares += fold(own * own)

    @pl.when(jnp.logical_not(has_lo))
    def _():
        v0[0:2] = jnp.zeros((2, nz, 2, rows, width), BF16)
        v1[0:2] = jnp.zeros((2, nz, 2, rows, width), BF16)
        th_side[0] = jnp.zeros((8, 128), F32)

    @pl.when(jnp.logical_not(has_hi))
    def _():
        v0[4:6] = jnp.zeros((2, nz, 2, rows, width), BF16)
        v1[4:6] = jnp.zeros((2, nz, 2, rows, width), BF16)
        th_side[1] = jnp.zeros((8, 128), F32)

    pl.semaphore_wait(
        barrier,
        1 + (nz - 1) + (INNER - 1) + (n_outer - 1)
        + lo_cross.astype(jnp.int32) + hi_cross.astype(jnp.int32),
    )

    order = []
    for d in range(1, nz // 2 + 1):
        order.append(d)
        if nz - d != d:
            order.append(nz - d)

    mid, low, high = pl.ds(2, 2), pl.ds(0, 2), pl.ds(4, 2)
    most = pl.ds(0, nz - 1)

    def gather(v, meanwhile=None):
        along = group(v.at[mid, most, c])
        along_in = {d: recvs.take() for d in order}
        down = group(v.at[mid, :, c], has_lo)
        up = group(v.at[mid, :, c], has_hi)
        pair = group(v.at[mid, :, c])
        pair_low = group(v.at[low, :, c], has_lo)
        pair_high = group(v.at[high, :, c], has_hi)
        own = v.at[mid, z, c]
        for d in reversed(order):
            send(own, own, (along[0], along_in[d], None), dev(s, at_z(d), c))
        for d in [0] + order:
            zz = at_z(nz - d) if d else z
            block = v.at[mid, zz, c]
            if d:
                arrive(block, along_in[d])
            send(block, v.at[high, zz, c], down, dev(s - 1, z, c))
            send(block, v.at[low, zz, c], up, dev(s + 1, z, c))
            send(block, block, pair, dev(s, z, other))
            if d == 0 and meanwhile is not None:
                meanwhile()
        arrive(v.at[low, :, c], up[1], has_lo)
        send(v.at[low, :, c], v.at[low, :, c], pair_low, dev(s, z, other))
        arrive(v.at[high, :, c], down[1], has_hi)
        send(v.at[high, :, c], v.at[high, :, c], pair_high, dev(s, z, other))
        arrive(v.at[mid, :, other], pair[1])
        arrive(v.at[low, :, other], pair_low[1], has_lo)
        arrive(v.at[high, :, other], pair_high[1], has_hi)

    def first_half(v, i):
        for k in range(terms):
            block = v[i + H - shifts_ref[k]].reshape(width, width)
            out = jnp.dot(left[k, i], block, preferred_element_type=F32)
            mixed[:, k * width : (k + 1) * width] = out.astype(BF16)

    def second_half(r, i):
        out = lax.dot_general(
            mixed[...], right[i], (((1,), (1,)), ((), ())), preferred_element_type=F32
        )
        total[r, i] = out.reshape(nz, 2, rows, width)
        return out

    def swap(r, i):
        pair = group(total.at[r, i, :, other])
        send(total.at[r, i, :, other], peer.at[r, i], pair, dev(s, z, other))
        return pair

    def scatter(r, i, pair, along):
        arrive(peer.at[r, i], pair[1])
        chunk[r, i] = (total[r, i, :, c] + peer[r, i]).astype(chunk.dtype)
        for d in reversed(order):
            zz = at_z(d)
            send(chunk.at[r, i, zz], landed.at[r, i, z], along, dev(s, zz, c))

    def collect(r, i):
        acc = total[r, i, z, c] + peer[r, i, z]
        for d in order:
            acc = acc + landed[r, i, at_z(nz - d)].astype(F32)
        return jnp.where(lives[i], acc, 0.0)

    def product(r, v, src):
        along = group(chunk.at[r, :, most])
        if r == 0:
            pltpu.make_async_copy(left_hbm, left, load_sem.at[1]).wait()
            pltpu.make_async_copy(right, right, load_sem.at[2]).wait()
        first_half(src, 0)
        out = second_half(r, 0)
        first = swap(r, 0)
        if r == 0:
            inner = fold(out * v0[2].reshape(width, width).astype(F32))
        first_half(src, 1)
        scatter(r, 0, first, along)
        out = second_half(r, 1)
        second = swap(r, 1)
        if r == 0:
            inner += fold(out * v0[3].reshape(width, width).astype(F32))
            theta_start(inner)
        scatter(r, 1, second, along)
        quotient = theta_column() if r == 0 else None
        arrive(landed.at[r, :, most], along[1])
        return [collect(r, i) for i in range(2)], quotient

    th_column = group(th_z.at[pl.ds(1, n_term - 1)])
    th_inner = group(th_x.at[pl.ds(1, INNER - 1)])
    th_outer = group(th_y.at[pl.ds(1, n_outer - 1)])
    th_down, th_up = group(th_own.at[1], has_lo), group(th_own.at[1], has_hi)

    def summed(own, slots, incoming):
        n = slots.shape[0]
        arrive(slots.at[pl.ds(1, n - 1)], incoming[1])
        return functools.reduce(jnp.add, [slots[d] for d in range(1, n)], own)

    def ratio(both):
        return jnp.sum(both[:4], keepdims=True) / jnp.sum(both[4:], keepdims=True)

    def column_ratio(both):
        value = ratio(both)
        return jnp.where(jnp.abs(value) < 1e30, value, 0.0)

    def theta_start(inner):
        th_own[0] = jnp.concatenate([inner[:4] + inner[4:], squares[:4] + squares[4:]], axis=0)
        for d in range(1, n_term):
            send(th_own.at[0], th_z.at[d], th_column, (s, lax.rem(t + d, n_term)))

    def theta_column():
        both = summed(th_own[0], th_z, th_column)
        th_own[1] = both
        for d in range(1, INNER):
            send(th_own.at[1], th_x.at[d], th_inner, (sy * INNER + lax.rem(sx + d, INNER), t))
        send(th_own.at[1], th_side.at[1], th_down, dev(s - 1, z, c))
        send(th_own.at[1], th_side.at[0], th_up, dev(s + 1, z, c))
        return column_ratio(both)

    def theta_across():
        th_own[2] = summed(th_own[1], th_x, th_inner)
        for d in range(1, n_outer):
            send(th_own.at[2], th_y.at[d], th_outer, (lax.rem(sy + d, n_outer) * INNER + sx, t))

    def theta_end():
        theta = ratio(summed(th_own[2], th_y, th_outer))
        arrive(th_side.at[0], th_up[1], has_lo)
        arrive(th_side.at[1], th_down[1], has_hi)
        return theta, column_ratio(th_side[0]), column_ratio(th_side[1])
    gather(v0)
    sigma, quotient = product(0, v0, v0)
    for i in range(2):
        outs[0, i] = sigma[i]
        psi = v0[2 + i, z, c].astype(F32)
        v1[2 + i, z, c] = (sigma[i] - quotient * psi).astype(BF16)
    sigma_out = pltpu.make_async_copy(outs.at[0], sigma_hbm, load_sem.at[0])
    sigma_out.start()
    gather(v1, theta_across)
    theta, below, above = theta_end()
    for j in range(6):
        change = (below, quotient, above)[j // 2] - theta
        v2[j] = (v1[j].astype(F32) + change * v0[j].astype(F32)).astype(BF16)
    last, _ = product(1, v1, v2)
    for i in range(2):
        outs[1, i] = last[i]
    next_out = pltpu.make_async_copy(outs.at[1], next_hbm, load_sem.at[1])
    next_out.start()
    sigma_out.wait()
    next_out.wait()
    for copy, when in sent:
        guarded(when, copy.wait_send)


def solution(mesh, link=BF16):
    dims = (mesh.shape["sector"], mesh.shape["term"])

    def step(psi, sizes, shifts, left, right):
        n_sector, n_term = dims
        nz = n_term // 2
        terms, width, rows = left.shape[0], left.shape[-1], psi.shape[1]
        n_send, n_recv = 2 * 9 + 5, 2 * (9 + nz - 1) + 5
        out = jax.ShapeDtypeStruct((2, rows, width), F32)
        smem = pl.BlockSpec(memory_space=pltpu.SMEM)
        hbm = pl.BlockSpec(memory_space=pl.ANY)
        return pl.pallas_call(
            functools.partial(kernel, dims),
            out_shape=(out, out),
            in_specs=[hbm, smem, smem, hbm, hbm],
            out_specs=(hbm, hbm),
            scratch_shapes=[
                pltpu.VMEM((2, rows, width), BF16),
                pltpu.VMEM((2, 2, rows, width), F32),
                pltpu.VMEM((terms, 2, width, width), BF16),
                pltpu.VMEM((2, width, terms * width), BF16),
                pltpu.VMEM((6, nz, 2, rows, width), BF16),
                pltpu.VMEM((6, nz, 2, rows, width), BF16),
                pltpu.VMEM((6, nz, 2, rows, width), BF16),
                pltpu.VMEM((width, terms * width), BF16),
                pltpu.VMEM((2, 2, nz, 2, rows, width), F32),
                pltpu.VMEM((2, 2, nz, rows, width), F32),
                pltpu.VMEM((2, 2, nz, rows, width), link),
                pltpu.VMEM((2, 2, nz, rows, width), link),
                pltpu.VMEM((3, 8, 128), F32),
                pltpu.VMEM((n_term, 8, 128), F32),
                pltpu.VMEM((INNER, 8, 128), F32),
                pltpu.VMEM((n_sector // INNER, 8, 128), F32),
                pltpu.VMEM((2, 8, 128), F32),
                pltpu.SemaphoreType.DMA((3,)),
                pltpu.SemaphoreType.DMA((n_send,)),
                pltpu.SemaphoreType.DMA((n_recv,)),
            ],
            compiler_params=pltpu.CompilerParams(
                collective_id=0, has_side_effects=True, vmem_limit_bytes=62 * 2**20
            ),
            cost_estimate=pl.CostEstimate(
                flops=8 * terms * width**3 * 2, bytes_accessed=4 * terms * width * width * 2,
                transcendentals=0,
            ),
        )(psi, sizes, shifts, left, right)

    return jax.shard_map(
        step,
        mesh=mesh,
        in_specs=(
            P("sector", "term", None),
            P("sector", None),
            P("term"),
            P("term", "sector", None, None),
            P("term", "sector", None, None),
        ),
        out_specs=(P("sector", "term", None), P("sector", "term", None)),
        check_vma=False,
    )
```

```python
import functools

import jax
import jax.numpy as jnp
from jax import lax
from jax.experimental import pallas as pl
from jax.experimental.pallas import tpu as pltpu
from jax.sharding import PartitionSpec as P

H = 2
MESH = pl.DeviceIdType.MESH
F32, BF16 = jnp.float32, jnp.bfloat16
INNER = 4


class Sems:
    def __init__(self, sems):
        self.sems, self.count = sems, 0

    def take(self):
        self.count += 1
        return self.sems.at[self.count - 1]


def kernel(
    dims, psi_hbm, sizes_hbm, shifts_hbm, left_hbm, right_hbm, out_hbm,
    psi_ref, sizes_ref, shifts_ref, outs, left, right, v0, v1, v2, mixed, total, peer, chunk, landed,
    th_own, th_z, th_x, th_y, th_side, load_sem, send_sem, recv_sem,
):
    n_sector, n_term = dims
    nz = n_term // 2
    n_outer = n_sector // INNER
    terms, width = left.shape[0], left.shape[-1]
    rows = psi_ref.shape[1]
    s, t = lax.axis_index("sector"), lax.axis_index("term")
    z, c = t // 2, t % 2
    sx, sy = s % INNER, s // INNER
    other = 1 - c
    has_lo, has_hi = s > 0, s < n_sector - 1
    sends, recvs = Sems(send_sem), Sems(recv_sem)
    sent = []

    def at_z(d):
        return lax.rem(z + d, nz)

    def dev(sector, zz, core):
        return (sector, zz * 2 + core)

    def guarded(when, act):
        if when is None:
            act()
        else:
            pl.when(when)(act)

    def remote(src, dst, out_sem, in_sem, device):
        return pltpu.make_async_remote_copy(
            src_ref=src, dst_ref=dst, send_sem=out_sem, recv_sem=in_sem,
            device_id=device, device_id_type=MESH,
        )

    def send(src, dst, group, device):
        out_sem, in_sem, when = group
        guarded(when, remote(src, dst, out_sem, in_sem, device).start)

    def group(region, when=None):
        out_sem, in_sem = sends.take(), recvs.take()
        sent.append((remote(region, region, out_sem, in_sem, dev(s, z, other)), when))
        return out_sem, in_sem, when

    def arrive(region, in_sem, when=None):
        copy = remote(region, region, send_sem.at[0], in_sem, dev(s, z, other))
        guarded(when, copy.wait_recv)

    own_load = pltpu.make_async_copy(psi_hbm, psi_ref, load_sem.at[0])
    own_load.start()
    sizes_load = pltpu.make_async_copy(sizes_hbm, sizes_ref, load_sem.at[3])
    shifts_load = pltpu.make_async_copy(shifts_hbm, shifts_ref, load_sem.at[4])
    sizes_load.start()
    shifts_load.start()
    pltpu.make_async_copy(left_hbm, left, load_sem.at[1]).start()
    for k in range(terms):
        for i in range(2):
            pltpu.make_async_copy(
                right_hbm.at[k, i], right.at[i, :, pl.ds(k * width, width)], load_sem.at[2]
            ).start()

    barrier = pltpu.get_barrier_semaphore()

    def greet(device):
        pl.semaphore_signal(barrier, inc=1, device_id=device, device_id_type=MESH)

    greet(dev(s, z, other))
    for d in range(1, nz):
        greet(dev(s, at_z(d), c))
    for d in range(1, INNER):
        greet(dev(sy * INNER + lax.rem(sx + d, INNER), z, c))
    for d in range(1, n_outer):
        greet(dev(lax.rem(sy + d, n_outer) * INNER + sx, z, c))
    lo_cross = jnp.logical_and(has_lo, sx == 0)
    hi_cross = jnp.logical_and(has_hi, sx == INNER - 1)
    pl.when(lo_cross)(lambda: greet(dev(s - 1, z, c)))
    pl.when(hi_cross)(lambda: greet(dev(s + 1, z, c)))

    def live(i):
        row = lax.broadcasted_iota(jnp.int32, (rows, width), 0) + t * rows
        col = lax.broadcasted_iota(jnp.int32, (rows, width), 1)
        return jnp.logical_and(row < sizes_ref[i, 0], col < sizes_ref[i, 1])

    sizes_load.wait()
    shifts_load.wait()
    own_load.wait()
    lives = [live(i) for i in range(2)]
    squares = jnp.zeros((8, 128), F32)

    def fold(x):
        x = x.reshape(-1, 8, width).sum(axis=0)
        return functools.reduce(jnp.add, [x[:, k : k + 128] for k in range(0, width, 128)])

    for i in range(2):
        own = jnp.where(lives[i], psi_ref[i].astype(F32), 0.0)
        v0[2 + i, z, c] = own.astype(BF16)
        squares += fold(own * own)

    @pl.when(jnp.logical_not(has_lo))
    def _():
        v0[0:2] = jnp.zeros((2, nz, 2, rows, width), BF16)
        v1[0:2] = jnp.zeros((2, nz, 2, rows, width), BF16)
        th_side[0] = jnp.zeros((8, 128), F32)

    @pl.when(jnp.logical_not(has_hi))
    def _():
        v0[4:6] = jnp.zeros((2, nz, 2, rows, width), BF16)
        v1[4:6] = jnp.zeros((2, nz, 2, rows, width), BF16)
        th_side[1] = jnp.zeros((8, 128), F32)

    pl.semaphore_wait(
        barrier,
        1 + (nz - 1) + (INNER - 1) + (n_outer - 1)
        + lo_cross.astype(jnp.int32) + hi_cross.astype(jnp.int32),
    )

    order = []
    for d in range(1, nz // 2 + 1):
        order.append(d)
        if nz - d != d:
            order.append(nz - d)

    mid, low, high = pl.ds(2, 2), pl.ds(0, 2), pl.ds(4, 2)
    most = pl.ds(0, nz - 1)

    def gather(v, meanwhile=None):
        along = group(v.at[mid, most, c])
        along_in = {d: recvs.take() for d in order}
        down = group(v.at[mid, :, c], has_lo)
        up = group(v.at[mid, :, c], has_hi)
        pair = group(v.at[mid, :, c])
        pair_low = group(v.at[low, :, c], has_lo)
        pair_high = group(v.at[high, :, c], has_hi)
        own = v.at[mid, z, c]
        for d in reversed(order):
            send(own, own, (along[0], along_in[d], None), dev(s, at_z(d), c))
        for d in [0] + order:
            zz = at_z(nz - d) if d else z
            block = v.at[mid, zz, c]
            if d:
                arrive(block, along_in[d])
            send(block, v.at[high, zz, c], down, dev(s - 1, z, c))
            send(block, v.at[low, zz, c], up, dev(s + 1, z, c))
            send(block, block, pair, dev(s, z, other))
            if d == 0 and meanwhile is not None:
                meanwhile()
        arrive(v.at[low, :, c], up[1], has_lo)
        send(v.at[low, :, c], v.at[low, :, c], pair_low, dev(s, z, other))
        arrive(v.at[high, :, c], down[1], has_hi)
        send(v.at[high, :, c], v.at[high, :, c], pair_high, dev(s, z, other))
        arrive(v.at[mid, :, other], pair[1])
        arrive(v.at[low, :, other], pair_low[1], has_lo)
        arrive(v.at[high, :, other], pair_high[1], has_hi)

    def first_half(v, i):
        for k in range(terms):
            block = v[i + H - shifts_ref[k]].reshape(width, width)
            out = jnp.dot(left[k, i], block, preferred_element_type=F32)
            mixed[:, k * width : (k + 1) * width] = out.astype(BF16)

    def second_half(r, i):
        out = lax.dot_general(
            mixed[...], right[i], (((1,), (1,)), ((), ())), preferred_element_type=F32
        )
        total[r, i] = out.reshape(nz, 2, rows, width)
        return out

    def swap(r, i):
        pair = group(total.at[r, i, :, other])
        send(total.at[r, i, :, other], peer.at[r, i], pair, dev(s, z, other))
        return pair

    def scatter(r, i, pair, along):
        arrive(peer.at[r, i], pair[1])
        chunk[r, i] = (total[r, i, :, c] + peer[r, i]).astype(chunk.dtype)
        for d in reversed(order):
            zz = at_z(d)
            send(chunk.at[r, i, zz], landed.at[r, i, z], along, dev(s, zz, c))

    def collect(r, i):
        acc = total[r, i, z, c] + peer[r, i, z]
        for d in order:
            acc = acc + landed[r, i, at_z(nz - d)].astype(F32)
        return jnp.where(lives[i], acc, 0.0)

    def product(r, v, src):
        along = group(chunk.at[r, :, most])
        if r == 0:
            pltpu.make_async_copy(left_hbm, left, load_sem.at[1]).wait()
            pltpu.make_async_copy(right, right, load_sem.at[2]).wait()
        first_half(src, 0)
        out = second_half(r, 0)
        first = swap(r, 0)
        if r == 0:
            inner = fold(out * v0[2].reshape(width, width).astype(F32))
        first_half(src, 1)
        scatter(r, 0, first, along)
        out = second_half(r, 1)
        second = swap(r, 1)
        if r == 0:
            inner += fold(out * v0[3].reshape(width, width).astype(F32))
            theta_start(inner)
        scatter(r, 1, second, along)
        quotient = theta_column() if r == 0 else None
        arrive(landed.at[r, :, most], along[1])
        return [collect(r, i) for i in range(2)], quotient

    th_column = group(th_z.at[pl.ds(1, n_term - 1)])
    th_inner = group(th_x.at[pl.ds(1, INNER - 1)])
    th_outer = group(th_y.at[pl.ds(1, n_outer - 1)])
    th_down, th_up = group(th_own.at[1], has_lo), group(th_own.at[1], has_hi)

    def summed(own, slots, incoming):
        n = slots.shape[0]
        arrive(slots.at[pl.ds(1, n - 1)], incoming[1])
        return functools.reduce(jnp.add, [slots[d] for d in range(1, n)], own)

    def ratio(both):
        return jnp.sum(both[:4], keepdims=True) / jnp.sum(both[4:], keepdims=True)

    def column_ratio(both):
        value = ratio(both)
        return jnp.where(jnp.abs(value) < 1e30, value, 0.0)

    def theta_start(inner):
        th_own[0] = jnp.concatenate([inner[:4] + inner[4:], squares[:4] + squares[4:]], axis=0)
        for d in range(1, n_term):
            send(th_own.at[0], th_z.at[d], th_column, (s, lax.rem(t + d, n_term)))

    def theta_column():
        both = summed(th_own[0], th_z, th_column)
        th_own[1] = both
        for d in range(1, INNER):
            send(th_own.at[1], th_x.at[d], th_inner, (sy * INNER + lax.rem(sx + d, INNER), t))
        send(th_own.at[1], th_side.at[1], th_down, dev(s - 1, z, c))
        send(th_own.at[1], th_side.at[0], th_up, dev(s + 1, z, c))
        return column_ratio(both)

    def theta_across():
        th_own[2] = summed(th_own[1], th_x, th_inner)
        for d in range(1, n_outer):
            send(th_own.at[2], th_y.at[d], th_outer, (lax.rem(sy + d, n_outer) * INNER + sx, t))

    def theta_end():
        theta = ratio(summed(th_own[2], th_y, th_outer))
        arrive(th_side.at[0], th_up[1], has_lo)
        arrive(th_side.at[1], th_down[1], has_hi)
        return theta, column_ratio(th_side[0]), column_ratio(th_side[1])
    gather(v0)
    sigma, quotient = product(0, v0, v0)
    for i in range(2):
        outs[0, i] = sigma[i]
        psi = v0[2 + i, z, c].astype(F32)
        v1[2 + i, z, c] = (sigma[i] - quotient * psi).astype(BF16)
    sigma_out = pltpu.make_async_copy(outs.at[0], out_hbm.at[0], load_sem.at[0])
    sigma_out.start()
    gather(v1, theta_across)
    theta, below, above = theta_end()
    for j in range(6):
        change = (below, quotient, above)[j // 2] - theta
        v2[j] = (v1[j].astype(F32) + change * v0[j].astype(F32)).astype(BF16)
    last, _ = product(1, v1, v2)
    for i in range(2):
        outs[1, i] = last[i]
    next_out = pltpu.make_async_copy(outs.at[1], out_hbm.at[1], load_sem.at[1])
    next_out.start()
    sigma_out.wait()
    next_out.wait()
    for copy, when in sent:
        guarded(when, copy.wait_send)


def solution(mesh, link=BF16):
    dims = (mesh.shape["sector"], mesh.shape["term"])

    def step(psi, sizes, shifts, left, right):
        n_sector, n_term = dims
        nz = n_term // 2
        terms, width, rows = left.shape[0], left.shape[-1], psi.shape[1]
        n_send, n_recv = 2 * 9 + 5, 2 * (9 + nz - 1) + 5
        out = jax.ShapeDtypeStruct((2, 2, rows, width), F32)
        hbm = pl.BlockSpec(memory_space=pl.ANY)
        both = pl.pallas_call(
            functools.partial(kernel, dims),
            out_shape=out,
            in_specs=[hbm] * 5,
            out_specs=hbm,
            scratch_shapes=[
                pltpu.VMEM((2, rows, width), BF16),
                pltpu.SMEM((2, 2), jnp.int32),
                pltpu.SMEM((terms,), jnp.int32),
                pltpu.VMEM((2, 2, rows, width), F32),
                pltpu.VMEM((terms, 2, width, width), BF16),
                pltpu.VMEM((2, width, terms * width), BF16),
                pltpu.VMEM((6, nz, 2, rows, width), BF16),
                pltpu.VMEM((6, nz, 2, rows, width), BF16),
                pltpu.VMEM((6, nz, 2, rows, width), BF16),
                pltpu.VMEM((width, terms * width), BF16),
                pltpu.VMEM((2, 2, nz, 2, rows, width), F32),
                pltpu.VMEM((2, 2, nz, rows, width), F32),
                pltpu.VMEM((2, 2, nz, rows, width), link),
                pltpu.VMEM((2, 2, nz, rows, width), link),
                pltpu.VMEM((3, 8, 128), F32),
                pltpu.VMEM((n_term, 8, 128), F32),
                pltpu.VMEM((INNER, 8, 128), F32),
                pltpu.VMEM((n_sector // INNER, 8, 128), F32),
                pltpu.VMEM((2, 8, 128), F32),
                pltpu.SemaphoreType.DMA((5,)),
                pltpu.SemaphoreType.DMA((n_send,)),
                pltpu.SemaphoreType.DMA((n_recv,)),
            ],
            compiler_params=pltpu.CompilerParams(
                collective_id=0, has_side_effects=True, vmem_limit_bytes=62 * 2**20
            ),
            cost_estimate=pl.CostEstimate(
                flops=8 * terms * width**3 * 2, bytes_accessed=4 * terms * width * width * 2,
                transcendentals=0,
            ),
        )(psi, sizes, shifts, left, right)
        return both[0], both[1]

    return jax.shard_map(
        step,
        mesh=mesh,
        in_specs=(
            P("sector", "term", None),
            P("sector", None),
            P("term"),
            P("term", "sector", None, None),
            P("term", "sector", None, None),
        ),
        out_specs=(P("sector", "term", None), P("sector", "term", None)),
        check_vma=False,
    )
```

```python
import functools

import jax
import jax.numpy as jnp
from jax import lax
from jax.experimental import pallas as pl
from jax.experimental.pallas import tpu as pltpu
from jax.sharding import PartitionSpec as P

H = 2
MESH = pl.DeviceIdType.MESH
F32, BF16 = jnp.float32, jnp.bfloat16
INNER = 4


class Sems:
    def __init__(self, sems):
        self.sems, self.count = sems, 0

    def take(self):
        self.count += 1
        return self.sems.at[self.count - 1]


def kernel(
    dims, psi_hbm, sizes_hbm, shifts_hbm, left_hbm, right_hbm, out_hbm,
    psi_ref, sizes_ref, shifts_ref, outs, left, right, v0, v1, v2, mixed, total, peer, chunk, landed,
    th_own, th_z, th_x, th_y, th_side, load_sem, send_sem, recv_sem,
):
    n_sector, n_term = dims
    nz = n_term // 2
    n_outer = n_sector // INNER
    terms, width = left.shape[0], left.shape[-1]
    rows = psi_ref.shape[1]
    s, t = lax.axis_index("sector"), lax.axis_index("term")
    z, c = t // 2, t % 2
    sx, sy = s % INNER, s // INNER
    other = 1 - c
    has_lo, has_hi = s > 0, s < n_sector - 1
    sends, recvs = Sems(send_sem), Sems(recv_sem)
    sent = []

    def at_z(d):
        return lax.rem(z + d, nz)

    def dev(sector, zz, core):
        return (sector, zz * 2 + core)

    def guarded(when, act):
        if when is None:
            act()
        else:
            pl.when(when)(act)

    def remote(src, dst, out_sem, in_sem, device):
        return pltpu.make_async_remote_copy(
            src_ref=src, dst_ref=dst, send_sem=out_sem, recv_sem=in_sem,
            device_id=device, device_id_type=MESH,
        )

    def send(src, dst, group, device):
        out_sem, in_sem, when = group
        guarded(when, remote(src, dst, out_sem, in_sem, device).start)

    def group(region, when=None):
        out_sem, in_sem = sends.take(), recvs.take()
        sent.append((remote(region, region, out_sem, in_sem, dev(s, z, other)), when))
        return out_sem, in_sem, when

    def arrive(region, in_sem, when=None):
        copy = remote(region, region, send_sem.at[0], in_sem, dev(s, z, other))
        guarded(when, copy.wait_recv)

    own_load = pltpu.make_async_copy(psi_hbm, psi_ref, load_sem.at[0])
    own_load.start()
    sizes_load = pltpu.make_async_copy(sizes_hbm, sizes_ref, load_sem.at[3])
    shifts_load = pltpu.make_async_copy(shifts_hbm, shifts_ref, load_sem.at[4])
    sizes_load.start()
    shifts_load.start()
    pltpu.make_async_copy(left_hbm, left, load_sem.at[1]).start()
    for k in range(terms):
        for i in range(2):
            pltpu.make_async_copy(
                right_hbm.at[k, i], right.at[i, :, pl.ds(k * width, width)], load_sem.at[2]
            ).start()

    barrier = pltpu.get_barrier_semaphore()

    def greet(device):
        pl.semaphore_signal(barrier, inc=1, device_id=device, device_id_type=MESH)

    greet(dev(s, z, other))
    for d in range(1, nz):
        greet(dev(s, at_z(d), c))
    for d in range(1, INNER):
        greet(dev(sy * INNER + lax.rem(sx + d, INNER), z, c))
    for d in range(1, n_outer):
        greet(dev(lax.rem(sy + d, n_outer) * INNER + sx, z, c))
    lo_cross = jnp.logical_and(has_lo, sx == 0)
    hi_cross = jnp.logical_and(has_hi, sx == INNER - 1)
    pl.when(lo_cross)(lambda: greet(dev(s - 1, z, c)))
    pl.when(hi_cross)(lambda: greet(dev(s + 1, z, c)))
    pl.when(has_lo)(lambda: greet(dev(s - 1, z, other)))
    pl.when(has_hi)(lambda: greet(dev(s + 1, z, other)))

    def live(i):
        row = lax.broadcasted_iota(jnp.int32, (rows, width), 0) + t * rows
        col = lax.broadcasted_iota(jnp.int32, (rows, width), 1)
        return jnp.logical_and(row < sizes_ref[i, 0], col < sizes_ref[i, 1])

    sizes_load.wait()
    shifts_load.wait()
    own_load.wait()
    lives = [live(i) for i in range(2)]
    squares = jnp.zeros((8, 128), F32)

    def fold(x):
        x = x.reshape(-1, 8, width).sum(axis=0)
        return functools.reduce(jnp.add, [x[:, k : k + 128] for k in range(0, width, 128)])

    for i in range(2):
        own = jnp.where(lives[i], psi_ref[i].astype(F32), 0.0)
        v0[2 + i, z, c] = own.astype(BF16)
        squares += fold(own * own)

    @pl.when(jnp.logical_not(has_lo))
    def _():
        v0[0:2] = jnp.zeros((2, nz, 2, rows, width), BF16)
        v1[0:2] = jnp.zeros((2, nz, 2, rows, width), BF16)
        th_side[0] = jnp.zeros((8, 128), F32)

    @pl.when(jnp.logical_not(has_hi))
    def _():
        v0[4:6] = jnp.zeros((2, nz, 2, rows, width), BF16)
        v1[4:6] = jnp.zeros((2, nz, 2, rows, width), BF16)
        th_side[1] = jnp.zeros((8, 128), F32)

    pl.semaphore_wait(
        barrier,
        1 + (nz - 1) + (INNER - 1) + (n_outer - 1)
        + lo_cross.astype(jnp.int32) + hi_cross.astype(jnp.int32)
        + has_lo.astype(jnp.int32) + has_hi.astype(jnp.int32),
    )

    order = []
    for d in range(1, nz // 2 + 1):
        order.append(d)
        if nz - d != d:
            order.append(nz - d)

    mid, low, high = pl.ds(2, 2), pl.ds(0, 2), pl.ds(4, 2)
    most = pl.ds(0, nz - 1)

    def gather(v, meanwhile=None):
        along = group(v.at[mid, most, c])
        along_in = {d: recvs.take() for d in order}
        near = [d for d in [0] + order if min(d, nz - d) < nz // 2 - 1]
        far = [d for d in order if d not in near]
        few, many = pl.ds(0, len(far)), pl.ds(0, len(near))
        pair = group(v.at[mid, :, c])
        sides = []
        for to, step, when_out, when_in in (
            (high, -1, has_lo, has_hi), (low, 1, has_hi, has_lo),
        ):
            sides.append((
                to, step, when_in,
                group(v.at[mid, many, c], when_out), group(v.at[mid, few, c], when_out),
                group(v.at[mid, few, c], when_out), group(v.at[to, many, c], when_in),
            ))
        own = v.at[mid, z, c]
        for d in reversed(order):
            send(own, own, (along[0], along_in[d], None), dev(s, at_z(d), c))

        def place(d):
            return at_z(nz - d) if d else z

        def cross():
            for to, _, when_in, narrow, _, _, shared in sides:
                arrive(v.at[to, many, c], narrow[1], when_in)
                for d in near:
                    block = v.at[to, place(d), c]
                    send(block, block, shared, dev(s, z, other))

        for d in near + far:
            block = v.at[mid, place(d), c]
            if d:
                arrive(block, along_in[d])
            for to, step, _, narrow, same, across, _ in sides:
                target = v.at[to, place(d), c]
                if d in near:
                    send(block, target, narrow, dev(s + step, z, c))
                else:
                    send(block, target, same, dev(s + step, z, c))
                    send(block, target, across, dev(s + step, z, other))
            send(block, block, pair, dev(s, z, other))
            if d == 0 and meanwhile is not None:
                meanwhile()
        cross()
        arrive(v.at[mid, :, other], pair[1])
        for to, _, when_in, _, same, across, shared in sides:
            arrive(v.at[to, many, other], shared[1], when_in)
            arrive(v.at[to, few, c], same[1], when_in)
            arrive(v.at[to, few, other], across[1], when_in)

    def first_half(v, i):
        for k in range(terms):
            block = v[i + H - shifts_ref[k]].reshape(width, width)
            out = jnp.dot(left[k, i], block, preferred_element_type=F32)
            mixed[:, k * width : (k + 1) * width] = out.astype(BF16)

    def second_half(r, i):
        out = lax.dot_general(
            mixed[...], right[i], (((1,), (1,)), ((), ())), preferred_element_type=F32
        )
        total[r, i] = out.reshape(nz, 2, rows, width)
        return out

    def swap(r, i):
        pair = group(total.at[r, i, :, other])
        send(total.at[r, i, :, other], peer.at[r, i], pair, dev(s, z, other))
        return pair

    def scatter(r, i, pair, along):
        arrive(peer.at[r, i], pair[1])
        chunk[r, i] = (total[r, i, :, c] + peer[r, i]).astype(chunk.dtype)
        for d in reversed(order):
            zz = at_z(d)
            send(chunk.at[r, i, zz], landed.at[r, i, z], along, dev(s, zz, c))

    def collect(r, i):
        acc = total[r, i, z, c] + peer[r, i, z]
        for d in order:
            acc = acc + landed[r, i, at_z(nz - d)].astype(F32)
        return jnp.where(lives[i], acc, 0.0)

    def product(r, v, src):
        along = group(chunk.at[r, :, most])
        if r == 0:
            pltpu.make_async_copy(left_hbm, left, load_sem.at[1]).wait()
            pltpu.make_async_copy(right, right, load_sem.at[2]).wait()
        first_half(src, 0)
        out = second_half(r, 0)
        first = swap(r, 0)
        if r == 0:
            inner = fold(out * v0[2].reshape(width, width).astype(F32))
        first_half(src, 1)
        scatter(r, 0, first, along)
        out = second_half(r, 1)
        second = swap(r, 1)
        if r == 0:
            inner += fold(out * v0[3].reshape(width, width).astype(F32))
            theta_start(inner)
        scatter(r, 1, second, along)
        quotient = theta_column() if r == 0 else None
        arrive(landed.at[r, :, most], along[1])
        return [collect(r, i) for i in range(2)], quotient

    th_column = group(th_z.at[pl.ds(1, n_term - 1)])
    th_inner = group(th_x.at[pl.ds(1, INNER - 1)])
    th_outer = group(th_y.at[pl.ds(1, n_outer - 1)])
    th_down, th_up = group(th_own.at[1], has_lo), group(th_own.at[1], has_hi)

    def summed(own, slots, incoming):
        n = slots.shape[0]
        arrive(slots.at[pl.ds(1, n - 1)], incoming[1])
        return functools.reduce(jnp.add, [slots[d] for d in range(1, n)], own)

    def ratio(both):
        return jnp.sum(both[:4], keepdims=True) / jnp.sum(both[4:], keepdims=True)

    def column_ratio(both):
        value = ratio(both)
        return jnp.where(jnp.abs(value) < 1e30, value, 0.0)

    def theta_start(inner):
        th_own[0] = jnp.concatenate([inner[:4] + inner[4:], squares[:4] + squares[4:]], axis=0)
        for d in range(1, n_term):
            send(th_own.at[0], th_z.at[d], th_column, (s, lax.rem(t + d, n_term)))

    def theta_column():
        both = summed(th_own[0], th_z, th_column)
        th_own[1] = both
        for d in range(1, INNER):
            send(th_own.at[1], th_x.at[d], th_inner, (sy * INNER + lax.rem(sx + d, INNER), t))
        send(th_own.at[1], th_side.at[1], th_down, dev(s - 1, z, c))
        send(th_own.at[1], th_side.at[0], th_up, dev(s + 1, z, c))
        return column_ratio(both)

    def theta_across():
        th_own[2] = summed(th_own[1], th_x, th_inner)
        for d in range(1, n_outer):
            send(th_own.at[2], th_y.at[d], th_outer, (lax.rem(sy + d, n_outer) * INNER + sx, t))

    def theta_end():
        theta = ratio(summed(th_own[2], th_y, th_outer))
        arrive(th_side.at[0], th_up[1], has_lo)
        arrive(th_side.at[1], th_down[1], has_hi)
        return theta, column_ratio(th_side[0]), column_ratio(th_side[1])
    gather(v0)
    sigma, quotient = product(0, v0, v0)
    for i in range(2):
        outs[0, i] = sigma[i]
        psi = v0[2 + i, z, c].astype(F32)
        v1[2 + i, z, c] = (sigma[i] - quotient * psi).astype(BF16)
    sigma_out = pltpu.make_async_copy(outs.at[0], out_hbm.at[0], load_sem.at[0])
    sigma_out.start()
    gather(v1, theta_across)
    theta, below, above = theta_end()
    for j in range(6):
        change = (below, quotient, above)[j // 2] - theta
        v2[j] = (v1[j].astype(F32) + change * v0[j].astype(F32)).astype(BF16)
    last, _ = product(1, v1, v2)
    for i in range(2):
        outs[1, i] = last[i]
    next_out = pltpu.make_async_copy(outs.at[1], out_hbm.at[1], load_sem.at[1])
    next_out.start()
    sigma_out.wait()
    next_out.wait()
    for copy, when in sent:
        guarded(when, copy.wait_send)


def solution(mesh, link=BF16):
    dims = (mesh.shape["sector"], mesh.shape["term"])

    def step(psi, sizes, shifts, left, right):
        n_sector, n_term = dims
        nz = n_term // 2
        terms, width, rows = left.shape[0], left.shape[-1], psi.shape[1]
        n_send, n_recv = 2 * 13 + 5, 2 * (13 + nz - 1) + 5
        out = jax.ShapeDtypeStruct((2, 2, rows, width), F32)
        hbm = pl.BlockSpec(memory_space=pl.ANY)
        both = pl.pallas_call(
            functools.partial(kernel, dims),
            out_shape=out,
            in_specs=[hbm] * 5,
            out_specs=hbm,
            scratch_shapes=[
                pltpu.VMEM((2, rows, width), BF16),
                pltpu.SMEM((2, 2), jnp.int32),
                pltpu.SMEM((terms,), jnp.int32),
                pltpu.VMEM((2, 2, rows, width), F32),
                pltpu.VMEM((terms, 2, width, width), BF16),
                pltpu.VMEM((2, width, terms * width), BF16),
                pltpu.VMEM((6, nz, 2, rows, width), BF16),
                pltpu.VMEM((6, nz, 2, rows, width), BF16),
                pltpu.VMEM((6, nz, 2, rows, width), BF16),
                pltpu.VMEM((width, terms * width), BF16),
                pltpu.VMEM((2, 2, nz, 2, rows, width), F32),
                pltpu.VMEM((2, 2, nz, rows, width), F32),
                pltpu.VMEM((2, 2, nz, rows, width), link),
                pltpu.VMEM((2, 2, nz, rows, width), link),
                pltpu.VMEM((3, 8, 128), F32),
                pltpu.VMEM((n_term, 8, 128), F32),
                pltpu.VMEM((INNER, 8, 128), F32),
                pltpu.VMEM((n_sector // INNER, 8, 128), F32),
                pltpu.VMEM((2, 8, 128), F32),
                pltpu.SemaphoreType.DMA((5,)),
                pltpu.SemaphoreType.DMA((n_send,)),
                pltpu.SemaphoreType.DMA((n_recv,)),
            ],
            compiler_params=pltpu.CompilerParams(
                collective_id=0, has_side_effects=True, vmem_limit_bytes=62 * 2**20
            ),
            cost_estimate=pl.CostEstimate(
                flops=8 * terms * width**3 * 2, bytes_accessed=4 * terms * width * width * 2,
                transcendentals=0,
            ),
        )(psi, sizes, shifts, left, right)
        return both[0], both[1]

    return jax.shard_map(
        step,
        mesh=mesh,
        in_specs=(
            P("sector", "term", None),
            P("sector", None),
            P("term"),
            P("term", "sector", None, None),
            P("term", "sector", None, None),
        ),
        out_specs=(P("sector", "term", None), P("sector", "term", None)),
        check_vma=False,
    )
```
